32 devices in a mesh: occ: 8 (over y, x, core), sym: 4 (over z).
Axes of the slice: x: 2, y: 2, z: 4, core: 2. Of those that a mesh axis runs over, the one named last changes fastest.
Arguments:
- hole_part: bfloat16 [32, 8], replicated, may hold values from -768 to 768
- hole_block: float32 [32, 32], replicated, may hold values from -0.0078125 to 0.0078125
- amplitudes: bfloat16 [1280, 8, 4, 256], P(('occ', 'sym')), may hold values from -6 to 6
- pair_first: int32 [1280], P(('occ', 'sym')), may hold values from 0 to 31, as said below
- pair_block: int32 [1280], P(('occ', 'sym')), may hold values from 0 to 7, as said below
- occ_tiles: bfloat16 [32, 32, 1024], P('occ'), may hold values from -0.0048828125 to 0.0048828125
- vir_tiles: bfloat16 [1024, 32, 256], P(None, 'occ'), may hold values from -0.1875 to 0.1875
- occ_energy: float32 [32], replicated, may hold values from -2 to -0.5
- vir_energy: float32 [256], replicated, may hold values from 0.25 to 3
Outputs:
- sigma_pairs: bfloat16 [1280, 8, 4, 256], P(('occ', 'sym'))
- sigma_hole: float32 [32, 8], replicated
The draws below stay inside these ranges and needn't reach their ends.
Inputs may be any that keep to these rules, and one draw needn't show every extreme that they name: `pair_first`: rows come in consecutive blocks of 40; in block b every value lies in [(b // 4) * 4, (b // 4) * 4 + 4). `pair_block`: rows come in consecutive blocks of 40; within one block no value is named by more than 5 rows. In every draw, for each s, all blocks b with b % 4 == s name one common value exactly 5 times.
All inputs are finite; a program needn't handle non-finite values.
Results may differ from the reference program's by a relative error of at most 0.0034.
Values may be sent and summed in bfloat16 or wider, within the bound.
A program may use at most 64 MiB of HBM per device.

```python
import jax
import jax.numpy as jnp
from jax import lax

OCC_DEV = 4
NGROUP = 8
NSTORE = 4
NO = 32
NVIRT = 256
NAUX = 1024
NVEC = 8
CAP = 5
PAIRS_DEV = 40
ROWS = 1280


def draw_pair_block(key, part):
    key = jax.random.fold_in(key, 11)
    hot_key, rest_key, order_key = jax.random.split(key, 3)
    blocks = NGROUP * NSTORE
    hot = jax.random.randint(hot_key, (NSTORE,), 0, NGROUP)
    hot_rows = jnp.tile(hot, NGROUP)
    rest_keys = jax.random.split(rest_key, blocks)
    spread = jax.vmap(lambda one: jax.random.permutation(one, CAP * (NGROUP - 1)))(rest_keys)
    spread = spread[:, :PAIRS_DEV - CAP]
    others = (hot_rows[:, None] + 1 + spread // CAP) % NGROUP
    named = jnp.concatenate([jnp.broadcast_to(hot_rows[:, None], (blocks, CAP)), others], axis=1)
    order_keys = jax.random.split(order_key, blocks)
    order = jax.vmap(lambda one: jax.random.permutation(one, PAIRS_DEV))(order_keys)
    named = jnp.take_along_axis(named, order, axis=1)
    return named.reshape(-1).astype(jnp.int32)


def draw_pair_first(key, part):
    key = jax.random.fold_in(key, 12)
    offset = jax.random.randint(key, (ROWS,), 0, OCC_DEV)
    group = jnp.arange(ROWS, dtype=jnp.int32) // (NSTORE * PAIRS_DEV)
    return (group * OCC_DEV + offset).astype(jnp.int32)


def steps_of(own_key, dims, pieces, smallest, high):
    gain = 1.0
    for axis_at, parts in pieces:
        heights = jax.random.uniform(jax.random.fold_in(jax.random.fold_in(own_key, 6), axis_at), (parts,), jnp.float32, smallest / len(pieces), high / len(pieces))
        gain = gain * jnp.repeat(jnp.exp(heights), dims[axis_at] // parts).reshape((-1,) + (1,) * (len(dims) - 1 - axis_at))
    return gain


def noise(stream_key, dims, deviation, reach, cuts=(), held_as=jnp.bfloat16):
    gain = steps_of(stream_key, dims, cuts, -0.22, 0.18) if cuts else 1.0
    values = jax.random.normal(stream_key, dims, jnp.float32) * deviation * gain
    return jnp.minimum(jnp.maximum(values, -reach), reach).astype(held_as)


def setup_inputs(seed: int = 0) -> dict:
    splits = jax.random.split(jax.random.key(seed), 10)
    return {
        "hole_part": noise(splits[0], (NO, NVEC), 128, 768.0),
        "hole_block": noise(splits[1], (NO, NO), (NO * 16384) ** -0.5, 0.0078125, (), jnp.float32),
        "amplitudes": noise(splits[2], (ROWS, NVEC, OCC_DEV, NVIRT), 1.0, 6.0, ((0, 32),)),
        "pair_first": draw_pair_first(jax.random.fold_in(splits[9], 71), 0),
        "pair_block": draw_pair_block(jax.random.fold_in(splits[9], 71), 0),
        "occ_tiles": noise(splits[5], (NO, NO, NAUX), (ROWS * NAUX) ** -0.5, 0.0048828125, ((0, 8),)),
        "vir_tiles": noise(splits[6], (NAUX, NO, NVIRT), NAUX ** -0.5, 0.1875, ((1, 8),)),
        "occ_energy": jnp.clip(jax.random.uniform(splits[7], (NO,), jnp.float32, -2.0, -0.5), -2.0, -0.5),
        "vir_energy": jnp.clip(jax.random.uniform(splits[8], (NVIRT,), jnp.float32, 0.25, 3.0), 0.25, 3.0),
    }


def reference(hole_part, hole_block, amplitudes, pair_first, pair_block, occ_tiles, vir_tiles, occ_energy, vir_energy):
    highest = lax.Precision.HIGHEST
    factors = jnp.einsum('kv,ikq->ivq', hole_part.astype(jnp.float32), occ_tiles.astype(jnp.float32), precision=highest).astype(jnp.bfloat16)
    coupled_all = jnp.dot(factors.reshape(NO * NVEC, NAUX), vir_tiles.reshape(NAUX, NO * NVIRT), preferred_element_type=jnp.float32)
    coupled_all = coupled_all.reshape(NO, NVEC, NGROUP, OCC_DEV * NVIRT)
    vir_wide = vir_tiles.astype(jnp.float32).reshape(NAUX, NGROUP, OCC_DEV * NVIRT)
    rows_group = PAIRS_DEV * NSTORE

    def per_group(group):
        start = (group * rows_group).astype(jnp.int32)
        amp_group = lax.dynamic_slice_in_dim(amplitudes, start, rows_group, 0)
        first_group = lax.dynamic_slice_in_dim(pair_first, start, rows_group, 0)
        block_group = lax.dynamic_slice_in_dim(pair_block, start, rows_group, 0)
        picked = coupled_all[first_group, :, block_group, :]
        couple = lax.optimization_barrier(picked.astype(jnp.bfloat16)).astype(jnp.float32)
        couple = couple.reshape(rows_group, NVEC, OCC_DEV, NVIRT)
        second = block_group[:, None] * OCC_DEV + jnp.arange(OCC_DEV, dtype=jnp.int32)[None, :]
        shift = vir_energy[None, None, None, :] - occ_energy[first_group][:, None, None, None] - occ_energy[second][:, None, :, None]
        sigma = (couple + shift * amp_group.astype(jnp.float32)).astype(jnp.bfloat16)
        local_first = first_group - group * OCC_DEV
        segment = (local_first * NGROUP + block_group).astype(jnp.int32)
        summed = jax.ops.segment_sum(amp_group.astype(jnp.float32).reshape(rows_group, NVEC, OCC_DEV * NVIRT), segment, num_segments=OCC_DEV * NGROUP)
        hole = jnp.einsum('ldvc,qdc->lvq', summed.reshape(OCC_DEV, NGROUP, NVEC, OCC_DEV * NVIRT), vir_wide, precision=highest)
        return sigma, hole

    sigmas, holes = lax.map(per_group, jnp.arange(NGROUP, dtype=jnp.int32))
    sigma_pairs = sigmas.reshape(ROWS, NVEC, OCC_DEV, NVIRT)
    hole_terms = holes.reshape(NO, NVEC, NAUX)
    sigma_hole = jnp.dot(hole_block, hole_part.astype(jnp.float32), precision=highest)
    sigma_hole = sigma_hole + jnp.einsum('ikq,ivq->kv', occ_tiles.astype(jnp.float32), hole_terms, precision=highest)
    return sigma_pairs, sigma_hole
```

```python
import functools

import jax
import jax.numpy as jnp
from jax import lax
from jax.experimental import pallas as pl
from jax.experimental.pallas import tpu as pltpu
from jax.sharding import PartitionSpec as P

MESH = pl.DeviceIdType.MESH
HIGHEST = lax.Precision.HIGHEST


def partner(me, step, count):
    if count & (count - 1):
        return lax.rem(me + step, count), lax.rem(me + count - step, count)
    other = me
    bit = 1
    while bit < count:
        if step & bit:
            other = other + bit * (1 - 2 * ((me // bit) % 2))
        bit *= 2
    return other, other


def kernel(
    n,
    ns,
    hole_ref,
    block_ref,
    x_ref,
    first_ref,
    dest_ref,
    occ_ref,
    vir_hbm,
    oe_ref,
    ve_ref,
    out_ref,
    hout_ref,
    vir,
    pick,
    pack,
    fac,
    got_a,
    got_f,
    cpl,
    cpl_home,
    back,
    back_home,
    red,
    red2,
    vsem,
    send_sem,
    recv_sem,
    zsend,
    zrecv,
):
    me = lax.axis_index("occ")
    own_z = lax.axis_index("sym")
    bo, no, aux = occ_ref.shape
    vec = hole_ref.shape[1]
    rows, cols = x_ref.shape
    virt = ve_ref.shape[1]
    pairs = first_ref.shape[1]
    part = bo * vec
    combos = n * part

    barrier = pltpu.get_barrier_semaphore()
    for j in range(1, n):
        pl.semaphore_signal(barrier, 1, device_id={"occ": partner(me, j, n)[0]}, device_id_type=MESH)
    for j in range(1, ns):
        pl.semaphore_signal(
            barrier, 1, device_id={"sym": partner(own_z, j, ns)[0]}, device_id_type=MESH
        )
    vcopy = pltpu.make_async_copy(vir_hbm, vir, vsem)
    vcopy.start()

    def rows_of(index):
        return pl.ds(pl.multiple_of(index * part, part), part)

    def copy_to(kind, j, src, dst):
        return pltpu.make_async_remote_copy(
            src_ref=src,
            dst_ref=dst,
            send_sem=send_sem.at[kind, j],
            recv_sem=recv_sem.at[kind, j],
            device_id={"occ": partner(me, j, n)[0]},
            device_id_type=MESH,
        )

    code = (dest_ref[...] * bo + first_ref[...] - me * bo).astype(jnp.float32)
    spread = (
        lax.broadcasted_iota(jnp.int32, (pairs, rows), 1) // vec
        == lax.broadcasted_iota(jnp.int32, (pairs, rows), 0)
    ).astype(jnp.bfloat16)
    code_row = jnp.dot(
        jnp.broadcast_to(code, (8, pairs)).astype(jnp.bfloat16),
        spread,
        preferred_element_type=jnp.float32,
    )[0:1, :].astype(jnp.int32)
    x_all = x_ref[...]
    r_it = lax.broadcasted_iota(jnp.int32, (combos, rows), 0)
    c_it = lax.broadcasted_iota(jnp.int32, (combos, rows), 1)
    pack_hot = ((r_it // vec == code_row) & (r_it % vec == c_it % vec)).astype(jnp.bfloat16)
    pick[...] = pack_hot

    chunk = min(combos, 256)
    for at in range(combos // chunk):
        hot = pick[at * chunk : (at + 1) * chunk, :]
        pack[at * chunk : (at + 1) * chunk, :] = jnp.dot(
            hot, x_all, preferred_element_type=jnp.float32
        ).astype(jnp.bfloat16)

    hole = hole_ref[...]
    parts = [
        lax.dot_general(
            hole, occ_ref[i], (((0,), (0,)), ((), ())), preferred_element_type=jnp.float32
        )
        for i in range(bo)
    ]
    fac[...] = jnp.concatenate(parts, axis=0).astype(jnp.bfloat16)

    pl.semaphore_wait(barrier, n - 1 + ns - 1)

    sends = []
    order = list(range(n - 1, 0, -1))
    for j in order:
        to, _ = partner(me, j, n)
        sends.append(copy_to(0, j, pack.at[rows_of(to)], got_a.at[rows_of(me)]))
        sends[-1].start()
    for j in order:
        sends.append(copy_to(1, j, fac, got_f.at[rows_of(me)]))
        sends[-1].start()
    got_a[rows_of(me), :] = pack[rows_of(me), :]
    got_f[rows_of(me), :] = fac[...]

    code_col = jnp.sum(
        jnp.where(
            lax.broadcasted_iota(jnp.int32, (rows, pairs), 0) // vec
            == lax.broadcasted_iota(jnp.int32, (rows, pairs), 1),
            jnp.broadcast_to(code, (rows, pairs)),
            0.0,
        ),
        axis=1,
        keepdims=True,
    ).astype(jnp.int32)
    orb = lax.broadcasted_iota(jnp.int32, (rows, no), 1)
    oe = jnp.broadcast_to(oe_ref[...], (rows, no))

    def energy_of(index):
        return jnp.sum(jnp.where(orb == index, oe, 0.0), axis=1, keepdims=True)

    dest_col = code_col // bo
    first_energy = energy_of(code_col - dest_col * bo + me * bo)
    second = [energy_of(dest_col * bo + m) for m in range(bo)]
    home_hot = (
        (lax.broadcasted_iota(jnp.int32, (rows, combos), 1) // vec == code_col)
        & (
            lax.broadcasted_iota(jnp.int32, (rows, combos), 1) % vec
            == lax.broadcasted_iota(jnp.int32, (rows, combos), 0) % vec
        )
    ).astype(jnp.bfloat16)

    vcopy.wait()
    tile = 256
    tiles = aux // tile
    for j in order:
        copy_to(0, j, pack.at[rows_of(me)], got_a.at[rows_of(partner(me, j, n)[1])]).wait_recv()

    for at in range(combos // chunk):
        here = slice(at * chunk, (at + 1) * chunk)

        def back_tile(t, carry, here=here):
            q = pl.ds(pl.multiple_of(t * tile, tile), tile)
            back[here, q] = lax.dot_general(
                got_a[here, :],
                vir[q, :],
                (((1,), (1,)), ((), ())),
                preferred_element_type=jnp.float32,
            ).astype(jnp.bfloat16)
            return carry

        lax.fori_loop(0, tiles, back_tile, 0)
    for j in order:
        to, _ = partner(me, j, n)
        sends.append(copy_to(2, j, back.at[rows_of(to)], back_home.at[rows_of(me)]))
        sends[-1].start()
    back_home[rows_of(me), :] = back[rows_of(me), :]

    for j in order:
        copy_to(1, j, fac, got_f.at[rows_of(partner(me, j, n)[1])]).wait_recv()
    for at in range(combos // chunk):
        here = slice(at * chunk, (at + 1) * chunk)

        def couple_tile(t, carry, here=here):
            c = pl.ds(pl.multiple_of(t * tile, tile), tile)
            cpl[here, c] = jnp.dot(
                got_f[here, :], vir[:, c], preferred_element_type=jnp.float32
            ).astype(jnp.bfloat16)
            return carry

        lax.fori_loop(0, cols // tile, couple_tile, 0)
    for j in order:
        to, _ = partner(me, j, n)
        sends.append(copy_to(3, j, cpl.at[rows_of(to)], cpl_home.at[rows_of(me)]))
        sends[-1].start()
    cpl_home[rows_of(me), :] = cpl[rows_of(me), :]

    for j in order:
        copy_to(2, j, back.at[rows_of(me)], back_home.at[rows_of(partner(me, j, n)[1])]).wait_recv()
    total = back_home[0:part, :].astype(jnp.float32)
    for d in range(1, n):
        total = total + back_home[d * part : (d + 1) * part, :].astype(jnp.float32)
    local = jnp.zeros((vec, no), jnp.float32)
    for i in range(bo):
        local = local + lax.dot_general(
            total[i * vec : (i + 1) * vec, :],
            occ_ref[i].astype(jnp.float32),
            (((1,), (1,)), ((), ())),
            precision=HIGHEST,
            preferred_element_type=jnp.float32,
        )
    lanes = red.shape[2]
    if lanes > no:
        local = jnp.concatenate([local, jnp.zeros((vec, lanes - no), jnp.float32)], axis=1)
    red[me] = local
    for j in order:
        sends.append(copy_to(4, j, red.at[me], red.at[me]))
        sends[-1].start()
    for j in order:
        copy_to(4, j, red.at[me], red.at[partner(me, j, n)[1]]).wait_recv()
    group = red[0]
    for d in range(1, n):
        group = group + red[d]
    red2[own_z] = group

    def copy_z(j, src, dst):
        return pltpu.make_async_remote_copy(
            src_ref=src,
            dst_ref=dst,
            send_sem=zsend.at[j],
            recv_sem=zrecv.at[j],
            device_id={"sym": partner(own_z, j, ns)[0]},
            device_id_type=MESH,
        )

    for j in range(1, ns):
        sends.append(copy_z(j, red2.at[own_z], red2.at[own_z]))
        sends[-1].start()

    for j in order:
        copy_to(3, j, cpl.at[rows_of(me)], cpl_home.at[rows_of(partner(me, j, n)[1])]).wait_recv()
    ve = ve_ref[...]
    for m in range(bo):
        c = slice(m * virt, (m + 1) * virt)
        coupled = jnp.dot(home_hot, cpl_home[:, c], preferred_element_type=jnp.float32)
        shift = ve - first_energy - second[m]
        out_ref[:, c] = (coupled + shift * x_ref[:, c].astype(jnp.float32)).astype(jnp.bfloat16)

    for j in range(1, ns):
        copy_z(j, red2.at[own_z], red2.at[partner(own_z, j, ns)[1]]).wait_recv()
    whole = red2[0]
    for s in range(1, ns):
        whole = whole + red2[s]
    direct = jnp.dot(
        block_ref[...],
        hole.astype(jnp.float32),
        precision=HIGHEST,
        preferred_element_type=jnp.float32,
    )
    hout_ref[...] = whole.T[0:no, :] + direct
    for copy in sends:
        copy.wait_send()


def body(
    hole_part,
    hole_block,
    amplitudes,
    pair_first,
    pair_block,
    occ_tiles,
    vir_tiles,
    occ_energy,
    vir_energy,
):
    n = lax.axis_size("occ")
    ns = lax.axis_size("sym")
    pairs, vec, bo, virt = amplitudes.shape
    aux = vir_tiles.shape[0]
    no = hole_part.shape[0]
    cols = bo * virt
    rows = pairs * vec
    part = bo * vec
    combos = n * part
    lanes = max(128, no)
    vmem = pl.BlockSpec(memory_space=pltpu.VMEM)
    half = jnp.bfloat16
    sigma, hole = pl.pallas_call(
        functools.partial(kernel, n, ns),
        out_shape=(
            jax.ShapeDtypeStruct((rows, cols), half),
            jax.ShapeDtypeStruct((no, vec), jnp.float32),
        ),
        in_specs=[vmem] * 6 + [pl.BlockSpec(memory_space=pl.ANY)] + [vmem] * 2,
        out_specs=(vmem, vmem),
        scratch_shapes=[
            pltpu.VMEM((aux, cols), half),
            pltpu.VMEM((combos, rows), half),
            pltpu.VMEM((combos, cols), half),
            pltpu.VMEM((part, aux), half),
            pltpu.VMEM((combos, cols), half),
            pltpu.VMEM((combos, aux), half),
            pltpu.VMEM((combos, cols), half),
            pltpu.VMEM((combos, cols), half),
            pltpu.VMEM((combos, aux), half),
            pltpu.VMEM((combos, aux), half),
            pltpu.VMEM((n, vec, lanes), jnp.float32),
            pltpu.VMEM((ns, vec, lanes), jnp.float32),
            pltpu.SemaphoreType.DMA,
            pltpu.SemaphoreType.DMA((5, n)),
            pltpu.SemaphoreType.DMA((5, n)),
            pltpu.SemaphoreType.DMA((ns,)),
            pltpu.SemaphoreType.DMA((ns,)),
        ],
        compiler_params=pltpu.CompilerParams(
            collective_id=0, has_side_effects=True, vmem_limit_bytes=44 * 1024 * 1024
        ),
        cost_estimate=pl.CostEstimate(
            flops=4 * combos * aux * cols, bytes_accessed=2 * aux * cols, transcendentals=0
        ),
    )(
        hole_part,
        hole_block,
        amplitudes.reshape(rows, cols),
        pair_first.reshape(1, pairs),
        pair_block.reshape(1, pairs),
        occ_tiles,
        vir_tiles.reshape(aux, cols),
        occ_energy.reshape(1, no),
        vir_energy.reshape(1, virt),
    )
    return sigma.reshape(amplitudes.shape), hole


def solution(mesh):
    placed = (
        P(),
        P(),
        P(("occ", "sym"), None, None, None),
        P(("occ", "sym")),
        P(("occ", "sym")),
        P("occ", None, None),
        P(None, "occ", None),
        P(),
        P(),
    )
    return jax.shard_map(
        body,
        mesh=mesh,
        in_specs=placed,
        out_specs=(P(("occ", "sym"), None, None, None), P()),
        check_vma=False,
    )
```

```python
import functools

import jax
import jax.numpy as jnp
from jax import lax
from jax.experimental import pallas as pl
from jax.experimental.pallas import tpu as pltpu
from jax.sharding import PartitionSpec as P

MESH = pl.DeviceIdType.MESH
HIGHEST = lax.Precision.HIGHEST


def partner(me, step, count):
    if count & (count - 1):
        return lax.rem(me + step, count), lax.rem(me + count - step, count)
    other = me
    bit = 1
    while bit < count:
        if step & bit:
            other = other + bit * (1 - 2 * ((me // bit) % 2))
        bit *= 2
    return other, other


def kernel(
    n,
    ns,
    hole_ref,
    block_ref,
    x_ref,
    first_ref,
    dest_ref,
    occ_ref,
    vir_hbm,
    oe_ref,
    ve_ref,
    out_ref,
    hout_ref,
    vir_raw,
    wide,
    vir,
    pick,
    pack,
    fac,
    got_a,
    got_f,
    cpl,
    cpl_home,
    back,
    back_home,
    red,
    red2,
    vsem,
    send_sem,
    recv_sem,
    zsend,
    zrecv,
):
    me = lax.axis_index("occ")
    own_z = lax.axis_index("sym")
    bo, no, aux = occ_ref.shape
    vec = hole_ref.shape[0]
    rows, cols = x_ref.shape
    virt = ve_ref.shape[1]
    pairs = first_ref.shape[1]
    part = bo * vec
    combos = n * part

    barrier = pltpu.get_barrier_semaphore()
    for j in range(1, n):
        pl.semaphore_signal(barrier, 1, device_id={"occ": partner(me, j, n)[0]}, device_id_type=MESH)
    for j in range(1, ns):
        pl.semaphore_signal(
            barrier, 1, device_id={"sym": partner(own_z, j, ns)[0]}, device_id_type=MESH
        )
    vcopy = pltpu.make_async_copy(vir_hbm, vir_raw, vsem)
    vcopy.start()

    def rows_of(index):
        return pl.ds(pl.multiple_of(index * part, part), part)

    def copy_to(kind, j, src, dst):
        return pltpu.make_async_remote_copy(
            src_ref=src,
            dst_ref=dst,
            send_sem=send_sem.at[kind, j],
            recv_sem=recv_sem.at[kind, j],
            device_id={"occ": partner(me, j, n)[0]},
            device_id_type=MESH,
        )

    code = (dest_ref[...] * bo + first_ref[...] - me * bo).astype(jnp.float32)
    spread = (
        lax.broadcasted_iota(jnp.int32, (1, rows), 1) // vec
        == lax.broadcasted_iota(jnp.int32, (pairs, rows), 0)
    ).astype(jnp.bfloat16)
    code_row = jnp.dot(
        jnp.broadcast_to(code, (8, pairs)).astype(jnp.bfloat16),
        spread,
        preferred_element_type=jnp.float32,
    )[0:1, :].astype(jnp.int32)
    x_all = x_ref[...]
    col_key = code_row * vec + lax.broadcasted_iota(jnp.int32, (1, rows), 1) % vec
    pack_hot = (lax.broadcasted_iota(jnp.int32, (combos, rows), 0) == col_key).astype(jnp.bfloat16)
    pick[...] = pack_hot

    chunk = min(combos, 256)
    for at in range(combos // chunk):
        hot = pick[at * chunk : (at + 1) * chunk, :]
        pack[at * chunk : (at + 1) * chunk, :] = jnp.dot(
            hot, x_all, preferred_element_type=jnp.float32
        ).astype(jnp.bfloat16)

    hole = hole_ref[...]
    parts = [
        jnp.dot(hole, occ_ref[i], preferred_element_type=jnp.float32) for i in range(bo)
    ]
    fac[...] = jnp.concatenate(parts, axis=0).astype(jnp.bfloat16)

    pl.semaphore_wait(barrier, n - 1 + ns - 1)

    sends = []
    order = list(range(n - 1, 0, -1))
    for j in order:
        to, _ = partner(me, j, n)
        sends.append(copy_to(0, j, pack.at[rows_of(to)], got_a.at[rows_of(me)]))
        sends[-1].start()
    for j in order:
        sends.append(copy_to(1, j, fac, got_f.at[rows_of(me)]))
        sends[-1].start()
    got_a[rows_of(me), :] = pack[rows_of(me), :]
    got_f[rows_of(me), :] = fac[...]

    code_col = jnp.sum(
        jnp.where(
            lax.broadcasted_iota(jnp.int32, (rows, 1), 0) // vec
            == lax.broadcasted_iota(jnp.int32, (rows, pairs), 1),
            jnp.broadcast_to(code, (rows, pairs)),
            0.0,
        ),
        axis=1,
        keepdims=True,
    ).astype(jnp.int32)
    orb = lax.broadcasted_iota(jnp.int32, (rows, no), 1)
    oe = jnp.broadcast_to(oe_ref[...], (rows, no))

    def energy_of(index):
        return jnp.sum(jnp.where(orb == index, oe, 0.0), axis=1, keepdims=True)

    dest_col = code_col // bo
    first_energy = energy_of(code_col - dest_col * bo + me * bo)
    second = [energy_of(dest_col * bo + m) for m in range(bo)]
    row_key = code_col * vec + lax.broadcasted_iota(jnp.int32, (rows, 1), 0) % vec
    home_hot = (lax.broadcasted_iota(jnp.int32, (rows, combos), 1) == row_key).astype(jnp.bfloat16)

    vcopy.wait()
    step = vir_raw.shape[0] // aux
    halves = step // bo
    lane = vir_raw.shape[1]
    some = wide.shape[1] // step

    def spread_rows(block, carry):
        slot = block % 2
        wide[slot] = vir_raw[
            pl.ds(pl.multiple_of(block * some * step, some * step), some * step), :
        ].astype(jnp.float32)
        here = pl.ds(pl.multiple_of(block * some, some), some)
        for t in range(halves):
            for m in range(bo):
                vir[here, m * virt + t * lane : m * virt + (t + 1) * lane] = wide[
                    slot, pl.ds(t * bo + m, some, stride=step), :
                ].astype(jnp.bfloat16)
        return carry

    lax.fori_loop(0, aux // some, spread_rows, 0)
    tile = 256
    tiles = aux // tile
    for j in order:
        copy_to(0, j, pack.at[rows_of(me)], got_a.at[rows_of(partner(me, j, n)[1])]).wait_recv()

    for at in range(combos // chunk):
        here = slice(at * chunk, (at + 1) * chunk)

        def back_tile(t, carry, here=here):
            q = pl.ds(pl.multiple_of(t * tile, tile), tile)
            back[here, q] = lax.dot_general(
                got_a[here, :],
                vir[q, :],
                (((1,), (1,)), ((), ())),
                preferred_element_type=jnp.float32,
            ).astype(jnp.bfloat16)
            return carry

        lax.fori_loop(0, tiles, back_tile, 0)
    for j in order:
        to, _ = partner(me, j, n)
        sends.append(copy_to(2, j, back.at[rows_of(to)], back_home.at[rows_of(me)]))
        sends[-1].start()
    back_home[rows_of(me), :] = back[rows_of(me), :]

    for j in order:
        copy_to(1, j, fac, got_f.at[rows_of(partner(me, j, n)[1])]).wait_recv()
    for at in range(combos // chunk):
        here = slice(at * chunk, (at + 1) * chunk)

        def couple_tile(t, carry, here=here):
            c = pl.ds(pl.multiple_of(t * tile, tile), tile)
            cpl[here, c] = jnp.dot(
                got_f[here, :], vir[:, c], preferred_element_type=jnp.float32
            ).astype(jnp.bfloat16)
            return carry

        lax.fori_loop(0, cols // tile, couple_tile, 0)
    for j in order:
        to, _ = partner(me, j, n)
        sends.append(copy_to(3, j, cpl.at[rows_of(to)], cpl_home.at[rows_of(me)]))
        sends[-1].start()
    cpl_home[rows_of(me), :] = cpl[rows_of(me), :]

    for j in order:
        copy_to(2, j, back.at[rows_of(me)], back_home.at[rows_of(partner(me, j, n)[1])]).wait_recv()
    total = back_home[0:part, :].astype(jnp.float32)
    for d in range(1, n):
        total = total + back_home[d * part : (d + 1) * part, :].astype(jnp.float32)
    local = jnp.zeros((vec, no), jnp.float32)
    for i in range(bo):
        local = local + lax.dot_general(
            total[i * vec : (i + 1) * vec, :],
            occ_ref[i].astype(jnp.float32),
            (((1,), (1,)), ((), ())),
            precision=HIGHEST,
            preferred_element_type=jnp.float32,
        )
    lanes = red.shape[2]
    if lanes > no:
        local = jnp.concatenate([local, jnp.zeros((vec, lanes - no), jnp.float32)], axis=1)
    red[me] = local
    for j in order:
        sends.append(copy_to(4, j, red.at[me], red.at[me]))
        sends[-1].start()
    for j in order:
        copy_to(4, j, red.at[me], red.at[partner(me, j, n)[1]]).wait_recv()
    group = red[0]
    for d in range(1, n):
        group = group + red[d]
    red2[own_z] = group

    def copy_z(j, src, dst):
        return pltpu.make_async_remote_copy(
            src_ref=src,
            dst_ref=dst,
            send_sem=zsend.at[j],
            recv_sem=zrecv.at[j],
            device_id={"sym": partner(own_z, j, ns)[0]},
            device_id_type=MESH,
        )

    for j in range(1, ns):
        sends.append(copy_z(j, red2.at[own_z], red2.at[own_z]))
        sends[-1].start()

    for j in order:
        copy_to(3, j, cpl.at[rows_of(me)], cpl_home.at[rows_of(partner(me, j, n)[1])]).wait_recv()
    ve = ve_ref[...]
    for m in range(bo):
        c = slice(m * virt, (m + 1) * virt)
        coupled = jnp.dot(home_hot, cpl_home[:, c], preferred_element_type=jnp.float32)
        shift = ve - first_energy - second[m]
        out_ref[:, c] = (coupled + shift * x_ref[:, c].astype(jnp.float32)).astype(jnp.bfloat16)

    for j in range(1, ns):
        copy_z(j, red2.at[own_z], red2.at[partner(own_z, j, ns)[1]]).wait_recv()
    whole = red2[0]
    for s in range(1, ns):
        whole = whole + red2[s]
    direct = lax.dot_general(
        hole.astype(jnp.float32),
        block_ref[...],
        (((1,), (1,)), ((), ())),
        precision=HIGHEST,
        preferred_element_type=jnp.float32,
    )
    hout_ref[...] = whole[:, 0:no] + direct
    for copy in sends:
        copy.wait_send()


def body(
    hole_part,
    hole_block,
    amplitudes,
    pair_first,
    pair_block,
    occ_tiles,
    vir_tiles,
    occ_energy,
    vir_energy,
):
    n = lax.axis_size("occ")
    ns = lax.axis_size("sym")
    pairs, vec, bo, virt = amplitudes.shape
    aux = vir_tiles.shape[0]
    no = hole_part.shape[0]
    cols = bo * virt
    rows = pairs * vec
    part = bo * vec
    combos = n * part
    lanes = max(128, no)
    vmem = pl.BlockSpec(memory_space=pltpu.VMEM)
    half = jnp.bfloat16
    sigma, hole = pl.pallas_call(
        functools.partial(kernel, n, ns),
        out_shape=(
            jax.ShapeDtypeStruct((rows, cols), half),
            jax.ShapeDtypeStruct((vec, no), jnp.float32),
        ),
        in_specs=[vmem] * 6 + [pl.BlockSpec(memory_space=pl.ANY)] + [vmem] * 2,
        out_specs=(vmem, vmem),
        scratch_shapes=[
            pltpu.VMEM((aux * cols // 128, 128), half),
            pltpu.VMEM((2, 64 * cols // 128, 128), jnp.float32),
            pltpu.VMEM((aux, cols), half),
            pltpu.VMEM((combos, rows), half),
            pltpu.VMEM((combos, cols), half),
            pltpu.VMEM((part, aux), half),
            pltpu.VMEM((combos, cols), half),
            pltpu.VMEM((combos, aux), half),
            pltpu.VMEM((combos, cols), half),
            pltpu.VMEM((combos, cols), half),
            pltpu.VMEM((combos, aux), half),
            pltpu.VMEM((combos, aux), half),
            pltpu.VMEM((n, vec, lanes), jnp.float32),
            pltpu.VMEM((ns, vec, lanes), jnp.float32),
            pltpu.SemaphoreType.DMA,
            pltpu.SemaphoreType.DMA((5, n)),
            pltpu.SemaphoreType.DMA((5, n)),
            pltpu.SemaphoreType.DMA((ns,)),
            pltpu.SemaphoreType.DMA((ns,)),
        ],
        compiler_params=pltpu.CompilerParams(
            collective_id=0, has_side_effects=True, vmem_limit_bytes=44 * 1024 * 1024
        ),
        cost_estimate=pl.CostEstimate(
            flops=4 * combos * aux * cols, bytes_accessed=2 * aux * cols, transcendentals=0
        ),
    )(
        hole_part.T,
        hole_block,
        amplitudes.reshape(rows, cols),
        pair_first.reshape(1, pairs),
        pair_block.reshape(1, pairs),
        occ_tiles,
        vir_tiles.reshape(aux, bo, virt // 128, 128)
        .transpose(0, 2, 1, 3)
        .reshape(aux * cols // 128, 128),
        occ_energy.reshape(1, no),
        vir_energy.reshape(1, virt),
    )
    return sigma.reshape(amplitudes.shape), hole.T


def solution(mesh):
    placed = (
        P(),
        P(),
        P(("occ", "sym"), None, None, None),
        P(("occ", "sym")),
        P(("occ", "sym")),
        P("occ", None, None),
        P(None, "occ", None),
        P(),
        P(),
    )
    return jax.shard_map(
        body,
        mesh=mesh,
        in_specs=placed,
        out_specs=(P(("occ", "sym"), None, None, None), P()),
        check_vma=False,
    )
```

```python
import functools

import jax
import jax.numpy as jnp
from jax import lax
from jax.experimental import pallas as pl
from jax.experimental.pallas import tpu as pltpu
from jax.sharding import PartitionSpec as P

MESH = pl.DeviceIdType.MESH
HIGHEST = lax.Precision.HIGHEST


def partner(me, step, count):
    if count & (count - 1):
        return lax.rem(me + step, count), lax.rem(me + count - step, count)
    other = me
    bit = 1
    while bit < count:
        if step & bit:
            other = other + bit * (1 - 2 * ((me // bit) % 2))
        bit *= 2
    return other, other


def kernel(
    n,
    ns,
    hole_hbm,
    block_hbm,
    x_ref,
    first_hbm,
    dest_hbm,
    occ_hbm,
    vir_hbm,
    oe_hbm,
    ve_hbm,
    out_ref,
    hout_ref,
    hole_ref,
    block_ref,
    first_ref,
    dest_ref,
    occ_ref,
    oe_ref,
    ve_ref,
    load_sem,
    vir_raw,
    wide,
    vir,
    pick,
    pack,
    fac,
    got_a,
    got_f,
    cpl,
    cpl_home,
    back,
    back_home,
    red,
    red2,
    vsem,
    send_sem,
    recv_sem,
    zsend,
    zrecv,
    zcsend,
    zcrecv,
):
    me = lax.axis_index("occ")
    own_z = lax.axis_index("sym")
    bo, no, aux = occ_ref.shape
    vec = hole_ref.shape[0]
    rows, cols = x_ref.shape
    virt = ve_ref.shape[1]
    pairs = first_ref.shape[1]
    part = bo * vec
    combos = n * part
    half = part // 2
    side = own_z % 2
    other_side = 1 - side

    barrier = pltpu.get_barrier_semaphore()
    for j in range(1, n):
        pl.semaphore_signal(barrier, 1, device_id={"occ": partner(me, j, n)[0]}, device_id_type=MESH)
    for j in range(1, ns):
        pl.semaphore_signal(
            barrier, 1, device_id={"sym": partner(own_z, j, ns)[0]}, device_id_type=MESH
        )
    vcopy = pltpu.make_async_copy(vir_hbm, vir_raw, vsem)
    loads = [
        pltpu.make_async_copy(src, dst, load_sem.at[at])
        for at, (src, dst) in enumerate(
            [
                (first_hbm, first_ref),
                (dest_hbm, dest_ref),
                (hole_hbm, hole_ref),
                (occ_hbm, occ_ref),
                (oe_hbm, oe_ref),
                (ve_hbm, ve_ref),
                (block_hbm, block_ref),
            ]
        )
    ]
    for load in loads:
        load.start()
    vcopy.start()
    loads[0].wait()
    loads[1].wait()

    def rows_of(index):
        return pl.ds(pl.multiple_of(index * part, part), part)

    def half_of(index):
        return pl.ds(pl.multiple_of(index * half, half), half)

    def copy_to(kind, j, src, dst):
        return pltpu.make_async_remote_copy(
            src_ref=src,
            dst_ref=dst,
            send_sem=send_sem.at[kind, j],
            recv_sem=recv_sem.at[kind, j],
            device_id={"occ": partner(me, j, n)[0]},
            device_id_type=MESH,
        )

    code = (dest_ref[...] * bo + first_ref[...] - me * bo).astype(jnp.float32)
    spread = (
        lax.broadcasted_iota(jnp.int32, (1, rows), 1) // vec
        == lax.broadcasted_iota(jnp.int32, (pairs, rows), 0)
    ).astype(jnp.bfloat16)
    code_row = jnp.dot(
        jnp.broadcast_to(code, (8, pairs)).astype(jnp.bfloat16),
        spread,
        preferred_element_type=jnp.float32,
    )[0:1, :].astype(jnp.int32)
    x_all = x_ref[...]
    col_key = code_row * vec + lax.broadcasted_iota(jnp.int32, (1, rows), 1) % vec
    pack_hot = (lax.broadcasted_iota(jnp.int32, (combos, rows), 0) == col_key).astype(jnp.bfloat16)
    pick[...] = pack_hot

    chunk = min(combos, 256)
    for at in range(combos // chunk):
        hot = pick[at * chunk : (at + 1) * chunk, :]
        pack[at * chunk : (at + 1) * chunk, :] = jnp.dot(
            hot, x_all, preferred_element_type=jnp.float32
        ).astype(jnp.bfloat16)

    loads[2].wait()
    loads[3].wait()
    hole = hole_ref[...]
    parts = [
        jnp.dot(hole, occ_ref[i], preferred_element_type=jnp.float32) for i in range(bo)
    ]
    fac[...] = jnp.concatenate(parts, axis=0).astype(jnp.bfloat16)

    pl.semaphore_wait(barrier, n - 1 + ns - 1)

    sends = []
    order = list(range(n - 1, 0, -1))
    for j in order:
        to, _ = partner(me, j, n)
        sends.append(copy_to(0, j, pack.at[rows_of(to)], got_a.at[rows_of(me)]))
        sends[-1].start()
    for j in order:
        sends.append(copy_to(1, j, fac.at[half_of(side)], got_f.at[half_of(me)]))
        sends[-1].start()
    got_a[rows_of(me), :] = pack[rows_of(me), :]
    got_f[half_of(me), :] = fac[half_of(side), :]

    code_col = jnp.sum(
        jnp.where(
            lax.broadcasted_iota(jnp.int32, (rows, 1), 0) // vec
            == lax.broadcasted_iota(jnp.int32, (rows, pairs), 1),
            jnp.broadcast_to(code, (rows, pairs)),
            0.0,
        ),
        axis=1,
        keepdims=True,
    ).astype(jnp.int32)
    for load in loads[4:]:
        load.wait()
    orb = lax.broadcasted_iota(jnp.int32, (rows, no), 1)
    oe = jnp.broadcast_to(oe_ref[...], (rows, no))

    def energy_of(index):
        return jnp.sum(jnp.where(orb == index, oe, 0.0), axis=1, keepdims=True)

    dest_col = code_col // bo
    first_energy = energy_of(code_col - dest_col * bo + me * bo)
    second = [energy_of(dest_col * bo + m) for m in range(bo)]
    row_key = code_col * vec + lax.broadcasted_iota(jnp.int32, (rows, 1), 0) % vec
    home_hot = (lax.broadcasted_iota(jnp.int32, (rows, combos), 1) == row_key).astype(jnp.bfloat16)

    vcopy.wait()
    step = vir_raw.shape[0] // aux
    halves = step // bo
    lane = vir_raw.shape[1]
    some = wide.shape[1] // step

    def spread_rows(block, carry):
        slot = block % 2
        wide[slot] = vir_raw[
            pl.ds(pl.multiple_of(block * some * step, some * step), some * step), :
        ].astype(jnp.float32)
        here = pl.ds(pl.multiple_of(block * some, some), some)
        for t in range(halves):
            for m in range(bo):
                vir[here, m * virt + t * lane : m * virt + (t + 1) * lane] = wide[
                    slot, pl.ds(t * bo + m, some, stride=step), :
                ].astype(jnp.bfloat16)
        return carry

    lax.fori_loop(0, aux // some, spread_rows, 0)
    tile = 256
    tiles = aux // tile
    for j in order:
        copy_to(0, j, pack.at[rows_of(me)], got_a.at[rows_of(partner(me, j, n)[1])]).wait_recv()

    for at in range(combos // chunk):
        here = slice(at * chunk, (at + 1) * chunk)

        def back_tile(t, carry, here=here):
            q = pl.ds(pl.multiple_of(t * tile, tile), tile)
            back[here, q] = lax.dot_general(
                got_a[here, :],
                vir[q, :],
                (((1,), (1,)), ((), ())),
                preferred_element_type=jnp.float32,
            ).astype(jnp.bfloat16)
            return carry

        lax.fori_loop(0, tiles, back_tile, 0)
    for j in order:
        to, _ = partner(me, j, n)
        sends.append(copy_to(2, j, back.at[rows_of(to)], back_home.at[rows_of(me)]))
        sends[-1].start()
    back_home[rows_of(me), :] = back[rows_of(me), :]

    for j in order:
        source = partner(me, j, n)[1]
        copy_to(1, j, fac.at[half_of(side)], got_f.at[half_of(source)]).wait_recv()
    thin = min(n * half, 256)
    for at in range(n * half // thin):
        here = slice(at * thin, (at + 1) * thin)

        def couple_tile(t, carry, here=here):
            c = pl.ds(pl.multiple_of(t * tile, tile), tile)
            cpl[here, c] = jnp.dot(
                got_f[here, :], vir[:, c], preferred_element_type=jnp.float32
            ).astype(jnp.bfloat16)
            return carry

        lax.fori_loop(0, cols // tile, couple_tile, 0)
    for j in order:
        to, _ = partner(me, j, n)
        sends.append(copy_to(3, j, cpl.at[half_of(to)], cpl_home.at[half_of(me * 2 + side)]))
        sends[-1].start()
    cpl_home[half_of(me * 2 + side), :] = cpl[half_of(me), :]

    def pass_on(j, rows):
        return pltpu.make_async_remote_copy(
            src_ref=cpl_home.at[rows],
            dst_ref=cpl_home.at[rows],
            send_sem=zcsend.at[j],
            recv_sem=zcrecv.at[j],
            device_id={"sym": own_z + 1 - 2 * side},
            device_id_type=MESH,
        )

    sends.append(pass_on(0, half_of(me * 2 + side)))
    sends[-1].start()

    for j in order:
        copy_to(2, j, back.at[rows_of(me)], back_home.at[rows_of(partner(me, j, n)[1])]).wait_recv()
    total = back_home[0:part, :].astype(jnp.float32)
    for d in range(1, n):
        total = total + back_home[d * part : (d + 1) * part, :].astype(jnp.float32)
    local = jnp.zeros((vec, no), jnp.float32)
    for i in range(bo):
        local = local + lax.dot_general(
            total[i * vec : (i + 1) * vec, :],
            occ_ref[i].astype(jnp.float32),
            (((1,), (1,)), ((), ())),
            precision=HIGHEST,
            preferred_element_type=jnp.float32,
        )
    lanes = red.shape[2]
    if lanes > no:
        local = jnp.concatenate([local, jnp.zeros((vec, lanes - no), jnp.float32)], axis=1)
    red[me] = local
    for j in order:
        sends.append(copy_to(4, j, red.at[me], red.at[me]))
        sends[-1].start()
    for j in order:
        rows_in = half_of(partner(me, j, n)[1] * 2 + side)
        copy_to(3, j, cpl.at[half_of(me)], cpl_home.at[rows_in]).wait_recv()
        sends.append(pass_on(j, rows_in))
        sends[-1].start()

    for j in order:
        copy_to(4, j, red.at[me], red.at[partner(me, j, n)[1]]).wait_recv()
    group = red[0]
    for d in range(1, n):
        group = group + red[d]
    red2[own_z] = group

    def copy_z(j, src, dst):
        return pltpu.make_async_remote_copy(
            src_ref=src,
            dst_ref=dst,
            send_sem=zsend.at[j],
            recv_sem=zrecv.at[j],
            device_id={"sym": partner(own_z, j, ns)[0]},
            device_id_type=MESH,
        )

    for j in range(1, ns):
        sends.append(copy_z(j, red2.at[own_z], red2.at[own_z]))
        sends[-1].start()

    pass_on(0, half_of(me * 2 + other_side)).wait_recv()
    for j in order:
        pass_on(j, half_of(partner(me, j, n)[1] * 2 + other_side)).wait_recv()
    ve = ve_ref[...]
    for m in range(bo):
        c = slice(m * virt, (m + 1) * virt)
        coupled = jnp.dot(home_hot, cpl_home[:, c], preferred_element_type=jnp.float32)
        shift = ve - first_energy - second[m]
        out_ref[:, c] = (coupled + shift * x_ref[:, c].astype(jnp.float32)).astype(jnp.bfloat16)

    for j in range(1, ns):
        copy_z(j, red2.at[own_z], red2.at[partner(own_z, j, ns)[1]]).wait_recv()
    whole = red2[0]
    for s in range(1, ns):
        whole = whole + red2[s]
    direct = lax.dot_general(
        hole.astype(jnp.float32),
        block_ref[...],
        (((1,), (1,)), ((), ())),
        precision=HIGHEST,
        preferred_element_type=jnp.float32,
    )
    hout_ref[...] = whole[:, 0:no] + direct
    for copy in sends:
        copy.wait_send()


def body(
    hole_part,
    hole_block,
    amplitudes,
    pair_first,
    pair_block,
    occ_tiles,
    vir_tiles,
    occ_energy,
    vir_energy,
):
    n = lax.axis_size("occ")
    ns = lax.axis_size("sym")
    pairs, vec, bo, virt = amplitudes.shape
    aux = vir_tiles.shape[0]
    no = hole_part.shape[0]
    cols = bo * virt
    rows = pairs * vec
    part = bo * vec
    combos = n * part
    lanes = max(128, no)
    vmem = pl.BlockSpec(memory_space=pltpu.VMEM)
    anywhere = pl.BlockSpec(memory_space=pl.ANY)
    half = jnp.bfloat16
    sigma, hole = pl.pallas_call(
        functools.partial(kernel, n, ns),
        out_shape=(
            jax.ShapeDtypeStruct((rows, cols), half),
            jax.ShapeDtypeStruct((vec, no), jnp.float32),
        ),
        in_specs=[anywhere] * 2 + [vmem] + [anywhere] * 6,
        out_specs=(vmem, vmem),
        scratch_shapes=[
            pltpu.VMEM((vec, no), half),
            pltpu.VMEM((no, no), jnp.float32),
            pltpu.VMEM((1, pairs), jnp.int32),
            pltpu.VMEM((1, pairs), jnp.int32),
            pltpu.VMEM((bo, no, aux), half),
            pltpu.VMEM((1, no), jnp.float32),
            pltpu.VMEM((1, virt), jnp.float32),
            pltpu.SemaphoreType.DMA((7,)),
            pltpu.VMEM((aux * cols // 128, 128), half),
            pltpu.VMEM((2, 64 * cols // 128, 128), jnp.float32),
            pltpu.VMEM((aux, cols), half),
            pltpu.VMEM((combos, rows), half),
            pltpu.VMEM((combos, cols), half),
            pltpu.VMEM((part, aux), half),
            pltpu.VMEM((combos, cols), half),
            pltpu.VMEM((combos // 2, aux), half),
            pltpu.VMEM((combos // 2, cols), half),
            pltpu.VMEM((combos, cols), half),
            pltpu.VMEM((combos, aux), half),
            pltpu.VMEM((combos, aux), half),
            pltpu.VMEM((n, vec, lanes), jnp.float32),
            pltpu.VMEM((ns, vec, lanes), jnp.float32),
            pltpu.SemaphoreType.DMA,
            pltpu.SemaphoreType.DMA((5, n)),
            pltpu.SemaphoreType.DMA((5, n)),
            pltpu.SemaphoreType.DMA((ns,)),
            pltpu.SemaphoreType.DMA((ns,)),
            pltpu.SemaphoreType.DMA((n,)),
            pltpu.SemaphoreType.DMA((n,)),
        ],
        compiler_params=pltpu.CompilerParams(
            collective_id=0, has_side_effects=True, vmem_limit_bytes=60 * 1024 * 1024
        ),
        cost_estimate=pl.CostEstimate(
            flops=4 * combos * aux * cols, bytes_accessed=2 * aux * cols, transcendentals=0
        ),
    )(
        hole_part.T,
        hole_block,
        amplitudes.reshape(rows, cols),
        pair_first.reshape(1, pairs),
        pair_block.reshape(1, pairs),
        occ_tiles,
        vir_tiles.reshape(aux, bo, virt // 128, 128)
        .transpose(0, 2, 1, 3)
        .reshape(aux * cols // 128, 128),
        occ_energy.reshape(1, no),
        vir_energy.reshape(1, virt),
    )
    return sigma.reshape(amplitudes.shape), hole.T


def solution(mesh):
    placed = (
        P(),
        P(),
        P(("occ", "sym"), None, None, None),
        P(("occ", "sym")),
        P(("occ", "sym")),
        P("occ", None, None),
        P(None, "occ", None),
        P(),
        P(),
    )
    return jax.shard_map(
        body,
        mesh=mesh,
        in_specs=placed,
        out_specs=(P(("occ", "sym"), None, None, None), P()),
        check_vma=False,
    )
```
